32 devices in a mesh: grp: 2 (over x), wf: 16 (over z, y, core).
Axes of the slice: x: 2, y: 2, z: 4, core: 2. Of those that a mesh axis runs over, the one named last changes fastest.
Arguments:
- vectors: bfloat16 [2, 256, 128, 128], P(None, ('grp', 'wf')), parts along dimension 1, may hold values from -16 to 16
- left_env: bfloat16 [21, 256, 128, 128], P(None, ('grp', 'wf')), parts along dimension 1, may hold values from -1 to 1
- right_env: bfloat16 [21, 256, 128, 128], P(None, ('grp', 'wf')), parts along dimension 1, may hold values from -2 to 2
- labels: int32 [256, 2], P(('grp', 'wf')), parts along dimension 0, may hold values from -3 to 3
- partner: int32 [8, 256], P(None, 'grp'), parts along dimension 1, may hold values from 0 to 127, as said below
- active: int32 [21, 256], P(None, ('grp', 'wf')), parts along dimension 1, may hold values 0 or 1
Outputs:
- residual: bfloat16 [2, 256, 128, 128], P(None, ('grp', 'wf')), parts along dimension 1
- rayleigh: float32 [4], P('grp'), parts along dimension 0
The draws below stay inside these ranges and needn't reach their ends.
There are 2 independent parts, one for each index of `grp`. The reference program is written for one: setup_inputs(seed, part) draws one part's arguments, and reference() takes and returns one part's arrays. A program takes and returns all parts, laid end to end along the dimension named above; each array names one. Nothing has to cross between parts.
Inputs may be any that keep to these rules, and one draw needn't show every extreme that they name: For every shift g, partner[g] is a permutation of the 128 block indices that keeps each block's slot: partner[g, q] mod 8 = q mod 8. Block q is held by device q // 8. Counted over all shifts and slots, the blocks of one device go to blocks of any one device at most 4 times, and some pair of devices reaches it.
All inputs are finite; a program needn't handle non-finite values. No bound on the sum of `active` on one device may be relied on, other than what follows from the above.
Results may differ from the reference program's by a relative error of at most 0.0043.
Values may be sent and summed in bfloat16 or wider, within the bound.
A program may use at most 128 MiB of HBM per device.

```python
import math
import jax
import jax.numpy as jnp
from jax import lax

BLK = 128
CAP = 8
GROUPS = 8
TERMS = 21
VECS = 2
NB = 128
N_WF = 16


def draw_vectors(key, part):
    key = jax.random.fold_in(key, 5)
    key_base, key_columns, key_common = jax.random.split(key, 3)
    position = (jnp.arange(NB, dtype=jnp.float32) + 0.5) / NB
    values = jax.random.normal(key_base, (VECS, NB, BLK, BLK), jnp.float32)
    values = values + 0.8 * jax.random.normal(key_common, (VECS, 1, BLK, BLK), jnp.float32)
    row_scale = 0.1 * 10.0 ** position
    column_scale = jnp.exp(jax.random.uniform(key_columns, (VECS, NB, 1, BLK), jnp.float32, math.log(0.5), math.log(5.0)))
    return jnp.clip(values * row_scale[None, :, None, None] * column_scale, -16.0, 16.0).astype(jnp.bfloat16)


def environment_blocks(key, diagonal_part, spread, bound):
    shape = (TERMS, NB, BLK, BLK)
    jitter = jax.random.normal(key, shape, jnp.float32)
    values = diagonal_part * jnp.eye(BLK, dtype=jnp.float32) + spread * jitter
    return jnp.clip(values, -bound, bound)


def draw_left_env(key, part):
    key = jax.random.fold_in(key, 11)
    spread = float(BLK * TERMS) ** (-0.5)
    return environment_blocks(key, 0.3, spread, 1.0).astype(jnp.bfloat16)


def draw_right_env(key, part):
    key = jax.random.fold_in(key, 13)
    spread = float(BLK) ** (-0.5)
    return environment_blocks(key, 0.5, spread, 2.0).astype(jnp.bfloat16)


def draw_partner(key, part):
    key = jax.random.fold_in(key, 7)
    key_order, key_relabel = jax.random.split(key)
    pair_count = GROUPS * CAP
    span_size = max(pair_count, N_WF)
    ordering = jax.random.permutation(key_order, span_size)[:pair_count]
    offsets = (ordering % N_WF).reshape(GROUPS, CAP)
    relabel = jax.random.permutation(key_relabel, N_WF)
    position = jnp.argsort(relabel)
    device = jnp.arange(NB, dtype=jnp.int32) // CAP
    slot_index = jnp.arange(NB, dtype=jnp.int32) % CAP
    target = relabel[(position[device][None, :] + offsets[:, slot_index]) % N_WF]
    return (target * CAP + slot_index[None, :]).astype(jnp.int32)


def with_ends(drawn, stream_key, low, high):
    longest = drawn.shape.index(max(drawn.shape))
    spots = []
    for shift in (0, 1):
        where = [jax.random.randint(jax.random.fold_in(stream_key, axis), (), 0, length) for axis, length in enumerate(drawn.shape)]
        where[longest] = (where[longest] + shift) % drawn.shape[longest]
        spots.append(tuple(where))
    return drawn.at[spots[0]].set(low).at[spots[1]].set(high)


def setup_inputs(seed: int = 0, part: int = 0) -> dict:
    streams_of = jax.random.split(jax.random.key(seed), 7)
    own_keys = jax.random.split(jax.random.fold_in(streams_of[6], part), 7)
    vectors = draw_vectors(jax.random.fold_in(jax.random.fold_in(streams_of[6], part), 71), part)
    left_env = draw_left_env(jax.random.fold_in(jax.random.fold_in(streams_of[6], part), 71), part)
    right_env = draw_right_env(jax.random.fold_in(jax.random.fold_in(streams_of[6], part), 71), part)
    labels = with_ends(jax.random.randint(own_keys[3], (NB, 2), -3, 4), jax.random.fold_in(own_keys[3], 1), -3, 3).astype(jnp.int32)
    partner = draw_partner(jax.random.fold_in(jax.random.fold_in(streams_of[6], part), 71), part)
    active = with_ends((jax.random.randint(own_keys[5], (TERMS, NB), 0, 8) < 7).astype(jnp.int32), jax.random.fold_in(own_keys[5], 1), 0, 1)
    return {"vectors": vectors, "left_env": left_env, "right_env": right_env, "labels": labels, "partner": partner, "active": active}


def reference(vectors, left_env, right_env, labels, partner, active):
    block_ids = jnp.arange(NB, dtype=jnp.int32)
    shift_ids = jnp.arange(GROUPS, dtype=jnp.int32)
    source = jnp.zeros((GROUPS, NB), jnp.int32).at[shift_ids[:, None], partner].set(
        jnp.broadcast_to(block_ids[None, :], (GROUPS, NB)))
    energy = 0.3 * (labels[:, 0] + 4).astype(jnp.float32) - 0.2 * labels[:, 1].astype(jnp.float32)
    floats = vectors.astype(jnp.float32)

    def apply_term(summed, term_index):
        anchor = source[term_index % GROUPS]
        right_block = right_env[term_index].astype(jnp.float32)
        carried = jnp.einsum("vqab,qbc->vqac", floats, right_block)
        carried = carried * active[term_index].astype(jnp.float32)[None, :, None, None]
        carried = lax.optimization_barrier(carried.astype(jnp.bfloat16)).astype(jnp.float32)
        relocated = jnp.take(carried, anchor, axis=1)
        left_block = left_env[term_index].astype(jnp.float32)
        return summed + jnp.einsum("qab,vqbc->vqac", left_block, relocated), None

    zero_start = jnp.zeros(floats.shape, jnp.float32)
    summed, _ = lax.scan(apply_term, zero_start, jnp.arange(TERMS, dtype=jnp.int32))
    image = summed + energy[None, :, None, None] * floats
    squares = jnp.sum(floats * floats, axis=(1, 2, 3))
    correlations = jnp.sum(floats * image, axis=(1, 2, 3))
    rayleigh = correlations / (squares + 1e-6)
    residual = (image - rayleigh[:, None, None, None] * floats).astype(jnp.bfloat16)
    return residual, rayleigh
```

```python
import functools

import jax
import jax.numpy as jnp
from jax import lax
from jax.experimental import pallas as pl
from jax.experimental.pallas import tpu as pltpu
from jax.sharding import PartitionSpec as P

VMEM_BYTES = 56 * 2**20


def term_parcel(flat_blocks, pack_rows, pack_keep, rows_out, per_shift):
    chosen = jnp.take(flat_blocks, pack_rows, axis=0)
    chosen = jnp.where(pack_keep[:, None, None], chosen, jnp.zeros((), chosen.dtype))
    return chosen.reshape((rows_out, per_shift) + flat_blocks.shape[1:])


def left_side(left_env, carried, vector, energy):
    summed = jnp.einsum("ksab,ksbc->sac", left_env, carried, preferred_element_type=jnp.float32)
    return summed + energy[:, None, None] * vector.astype(jnp.float32)


def per_device(vectors, left_env, right_env, labels, partner, active):
    node_count = lax.axis_size("wf")
    this_device = lax.axis_index("wf")
    vector_count = vectors.shape[0]
    slot_count = vectors.shape[1]
    block_side = vectors.shape[2]
    term_count = left_env.shape[0]
    shift_count = partner.shape[0]
    per_shift = (term_count + shift_count - 1) // shift_count
    peer_room = max(1, shift_count * slot_count // node_count)
    item_count = shift_count * slot_count
    rows_out = node_count * peer_room
    item_ids = jnp.arange(item_count, dtype=jnp.int32)
    slot_ids = jnp.arange(slot_count, dtype=jnp.int32)
    shift_ids = jnp.arange(shift_count, dtype=jnp.int32)
    own_targets = lax.dynamic_slice_in_dim(partner, this_device * slot_count, slot_count, 1)
    dest_device = (own_targets // slot_count).reshape(item_count)
    precedes = item_ids[None, :] < item_ids[:, None]
    order_rank = jnp.sum((dest_device[None, :] == dest_device[:, None]) & precedes, axis=1)
    place_device = jnp.arange(node_count, dtype=jnp.int32)[:, None, None]
    place_rank = jnp.arange(peer_room, dtype=jnp.int32)[None, :, None]
    matched = (dest_device[None, None, :] == place_device) & (
        order_rank[None, None, :] == place_rank
    )
    send_item = jnp.sum(jnp.where(matched, item_ids[None, None, :], 0), axis=2).reshape(rows_out)
    send_live = jnp.any(matched, axis=2).reshape(rows_out)
    own_blocks = this_device * slot_count + slot_ids
    block_ids = jnp.arange(partner.shape[1], dtype=jnp.int32)
    found_hits = partner[:, None, :] == own_blocks[None, :, None]
    anchor = jnp.sum(jnp.where(found_hits, block_ids[None, None, :], 0), axis=2)
    sender = anchor // slot_count
    cell_item = shift_ids[:, None] * slot_count + anchor % slot_count
    columns = sender[:, :, None] * slot_count + slot_ids[None, None, :]
    their_device = (
        jnp.take(partner, columns.reshape(-1), axis=1).reshape(
            shift_count, shift_count, slot_count, slot_count
        )
        // slot_count
    )
    their_item = shift_ids[:, None, None, None] * slot_count + slot_ids[None, None, None, :]
    before = their_item < cell_item[None, :, :, None]
    rank_cell = jnp.sum((their_device == this_device) & before, axis=(0, 3))
    recv_row = sender * peer_room + rank_cell
    term_ids = jnp.arange(term_count, dtype=jnp.int32)
    term_shift = term_ids % shift_count
    term_level = term_ids // shift_count
    level_ids = jnp.arange(per_shift, dtype=jnp.int32)
    term_grid = (send_item // slot_count)[:, None] + level_ids[None, :] * shift_count
    pack_rows = (
        jnp.minimum(term_grid, term_count - 1) * slot_count + (send_item % slot_count)[:, None]
    ).reshape(-1)
    pack_keep = (send_live[:, None] & (term_grid < term_count)).reshape(-1)
    unpack_rows = (recv_row[term_shift] * per_shift + term_level[:, None]).reshape(-1)
    energy = 0.3 * (labels[:, 0] + 4).astype(jnp.float32) - 0.2 * labels[:, 1].astype(jnp.float32)
    images = []
    keep_terms = active.astype(jnp.float32)[:, :, None, None]
    for vector_index in range(vector_count):
        product = jnp.einsum(
            "sab,ksbc->ksac", vectors[vector_index], right_env, preferred_element_type=jnp.float32
        )
        carried = (product * keep_terms).astype(jnp.bfloat16)
        parcel = term_parcel(
            carried.reshape(term_count * slot_count, block_side, block_side),
            pack_rows,
            pack_keep,
            rows_out,
            per_shift,
        )
        arrived = lax.all_to_all(parcel, "wf", split_axis=0, concat_axis=0, tiled=True)
        relocated = jnp.take(
            arrived.reshape(-1, block_side, block_side), unpack_rows, axis=0
        ).reshape(term_count, slot_count, block_side, block_side)
        images.append(left_side(left_env, relocated, vectors[vector_index], energy))
    image = jnp.stack(images)
    floats = vectors.astype(jnp.float32)
    squares = jnp.sum(floats * floats, axis=(1, 2, 3))
    correlations = jnp.sum(floats * image, axis=(1, 2, 3))
    squares_all, correlations_all = lax.psum((squares, correlations), "wf")
    rayleigh = correlations_all / (squares_all + 1e-06)
    residual = (image - rayleigh[:, None, None, None] * floats).astype(jnp.bfloat16)
    return (residual, rayleigh)


def ranked(hits, room):
    rank = jnp.cumsum(hits.astype(jnp.int32), axis=-1) - 1
    item_ids = jnp.arange(hits.shape[-1], dtype=jnp.int32)
    level = jnp.arange(room, dtype=jnp.int32)[:, None]
    matched = hits[..., None, :] & (rank[..., None, :] == level)
    return jnp.sum(jnp.where(matched, item_ids, 0), axis=-1)


def peer_of(me, step, nodes):
    difference = nodes - 1 - step
    peer, bit = 0, 1
    while bit < nodes:
        peer += ((me // bit + difference // bit) % 2) * bit
        bit *= 2
    return peer


def node_kernel(
    sizes,
    send_item,
    recv_cell,
    place,
    active,
    energy,
    v_ref,
    r_ref,
    l_hbm,
    out_ref,
    ray_ref,
    l_ref,
    vall,
    parcel,
    arrived,
    partial,
    images,
    stats,
    l_sem,
    v_recv,
    v_send,
    y_send,
    r_recv,
    r_send,
    s_recv,
    s_send,
):
    nodes, terms, shifts, slots, room, levels, side = sizes
    z_count = nodes // 4
    steps = nodes - 1
    me = lax.axis_index("wf")
    z, y, core = me // 4, (me // 2) % 2, me % 2
    l_copy = pltpu.make_async_copy(l_hbm, l_ref, l_sem)
    l_copy.start()

    barrier = pltpu.get_barrier_semaphore()

    def greet(step, carry):
        pl.semaphore_signal(barrier, inc=1, device_id={"wf": peer_of(me, step, nodes)})
        return carry

    lax.fori_loop(0, steps, greet, 0)
    pl.semaphore_wait(barrier, steps)

    def v_copy(chunk, target, send_sem):
        return pltpu.make_async_remote_copy(
            src_ref=vall.at[chunk],
            dst_ref=vall.at[chunk],
            send_sem=send_sem,
            recv_sem=v_recv.at[chunk],
            device_id={"wf": target},
        )

    y_peer = z * 4 + (1 - y) * 2 + core
    core_peer = z * 4 + y * 2 + (1 - core)
    up, down = (me + 4) % nodes, (me + nodes - 4) % nodes

    def wait_chunk(chunk):
        v_copy(chunk, core_peer, y_send.at[0]).wait_recv()

    def each_way(dz, action):
        index = dz + z_count - 1
        chunk = me + 4 * dz
        if dz <= 0:

            @pl.when(z < z_count - 1)
            def _():
                action(v_copy(chunk, up, v_send.at[index, 0]))

        if dz >= 0:

            @pl.when(z > 0)
            def _():
                action(v_copy(chunk, down, v_send.at[index, 1]))

        action(v_copy(chunk, y_peer, v_send.at[index, 2]))
        action(v_copy(chunk, core_peer, v_send.at[index, 3]))

    def y_chunk(z_step):
        return ((z + z_step) % z_count) * 4 + (1 - y) * 2 + core

    def r_copy(step):
        return pltpu.make_async_remote_copy(
            src_ref=parcel.at[step],
            dst_ref=arrived.at[step],
            send_sem=r_send.at[step],
            recv_sem=r_recv.at[step],
            device_id={"wf": peer_of(me, step, nodes)},
        )

    def pack(step, buffer):
        peer = peer_of(me, step, nodes)
        for index in range(room):
            item = send_item[peer * room + index]
            shift, slot = item // slots, item % slots
            for level in range(levels):
                term = shift + level * shifts
                live = (term < terms).astype(jnp.int32)
                term = jnp.minimum(term, terms - 1)
                keep = (active[term * slots + slot] * live).astype(jnp.float32)
                block = r_ref[term, slot].astype(jnp.float32) * keep
                buffer[step, index, level] = block.astype(jnp.bfloat16)

    def pack_and_send(step, carry):
        pack(step, parcel)
        r_copy(step).start()
        return carry

    vall[me] = v_ref[...]
    each_way(0, lambda copy: copy.start())
    lax.fori_loop(0, nodes // 2, pack_and_send, 0)

    def inside(dz):
        return (z + dz >= 0) & (z + dz < z_count)

    others = [sign * far for far in range(1, z_count) for sign in (-1, 1)]
    for dz in others:

        @pl.when(inside(dz))
        def _(dz=dz):
            wait_chunk(me + 4 * dz)
            each_way(dz, lambda copy: copy.start())

    lax.fori_loop(nodes // 2, steps, pack_and_send, 0)
    pack(steps, arrived)

    def pass_on(z_step, carry):
        chunk = y_chunk(z_step)
        wait_chunk(chunk)
        v_copy(chunk, core_peer, y_send.at[z_step]).start()
        return carry

    lax.fori_loop(0, z_count, pass_on, 0)

    def last_chunks(z_step, carry):
        z_from = (z + z_step) % z_count
        wait_chunk(z_from * 4 + y * 2 + (1 - core))
        wait_chunk(z_from * 4 + (1 - y) * 2 + (1 - core))
        return carry

    lax.fori_loop(0, z_count, last_chunks, 0)
    l_copy.wait()

    def multiply(step):
        peer = peer_of(me, step, nodes)

        def one(index, carry):
            cell = recv_cell[peer * room + index]
            shift, slot = cell // slots, cell % slots
            pair = jnp.concatenate([vall[peer, 0, slot], vall[peer, 1, slot]], axis=0)
            total = jnp.zeros((side, 2 * side), jnp.float32)
            for level in range(levels):
                term = jnp.minimum(shift + level * shifts, terms - 1)
                carried = jnp.dot(
                    pair, arrived[step, index, level], preferred_element_type=jnp.float32
                ).astype(jnp.bfloat16)
                both = jnp.concatenate([carried[:side], carried[side:]], axis=1)
                total += jnp.dot(l_ref[term, slot], both, preferred_element_type=jnp.float32)
            partial[step, index] = total
            return carry

        lax.fori_loop(0, room, one, 0)

    multiply(steps)

    def take(back, carry):
        step = steps - 1 - back
        r_copy(step).wait_recv()
        multiply(step)
        return carry

    lax.fori_loop(0, steps, take, 0)

    def total_slot(slot, carry):
        image = jnp.zeros((side, 2 * side), jnp.float32)
        for shift in range(shifts):
            spot = place[shift * slots + slot]
            image += partial[spot // room, spot % room]
        own = jnp.concatenate([v_ref[0, slot], v_ref[1, slot]], axis=1).astype(jnp.float32)
        image += energy[slot] * own
        images[slot] = image
        squares = jnp.sum(own * own, axis=0, keepdims=True)
        correlations = jnp.sum(own * image, axis=0, keepdims=True)
        return (carry[0] + squares, carry[1] + correlations)

    blank = jnp.zeros((1, 2 * side), jnp.float32)
    squares, correlations = lax.fori_loop(0, slots, total_slot, (blank, blank))
    row = lax.broadcasted_iota(jnp.int32, (8, 2 * side), 0)
    stats[me] = jnp.where(row == 0, squares, jnp.where(row == 1, correlations, 0.0))

    def s_copy(chunk, step):
        return pltpu.make_async_remote_copy(
            src_ref=stats.at[chunk],
            dst_ref=stats.at[chunk],
            send_sem=s_send.at[step],
            recv_sem=s_recv.at[chunk],
            device_id={"wf": peer_of(me, step, nodes)},
        )

    def share(step, carry):
        s_copy(me, step).start()
        return carry

    lax.fori_loop(0, steps, share, 0)

    def hear(step, carry):
        s_copy(peer_of(me, step, nodes), step).wait_recv()
        return carry

    lax.fori_loop(0, steps, hear, 0)
    sums = stats[0]
    for node in range(1, nodes):
        sums += stats[node]
    quotients = []
    for vector in range(2):
        lanes = slice(vector * side, (vector + 1) * side)
        square = jnp.sum(sums[0:1, lanes], axis=1, keepdims=True)
        correlation = jnp.sum(sums[1:2, lanes], axis=1, keepdims=True)
        quotient = correlation / (square + 1e-06)
        quotients.append(jnp.broadcast_to(quotient, (1, side)))
    ray_ref[...] = jnp.concatenate(quotients, axis=0)
    factor = jnp.concatenate(quotients, axis=1)

    def finish(slot, carry):
        own = jnp.concatenate([v_ref[0, slot], v_ref[1, slot]], axis=1).astype(jnp.float32)
        result = (images[slot] - factor * own).astype(jnp.bfloat16)
        out_ref[0, slot] = result[:, :side]
        out_ref[1, slot] = result[:, side:]
        return carry

    lax.fori_loop(0, slots, finish, 0)

    each_way(0, lambda copy: copy.wait_send())
    for dz in others:

        @pl.when(inside(dz))
        def _(dz=dz):
            each_way(dz, lambda copy: copy.wait_send())

    def sent_y(z_step, carry):
        v_copy(y_chunk(z_step), core_peer, y_send.at[z_step]).wait_send()
        return carry

    lax.fori_loop(0, z_count, sent_y, 0)

    def sent(step, carry):
        r_copy(step).wait_send()
        s_copy(me, step).wait_send()
        return carry

    lax.fori_loop(0, steps, sent, 0)


def node_program(vectors, left_env, right_env, labels, partner, active):
    nodes = lax.axis_size("wf")
    me = lax.axis_index("wf")
    count, slots, side = vectors.shape[:3]
    terms, shifts = left_env.shape[0], partner.shape[0]
    levels = (terms + shifts - 1) // shifts
    items = shifts * slots
    room = items // nodes
    node_ids = jnp.arange(nodes, dtype=jnp.int32)
    owner = (partner // slots).reshape(shifts, nodes, slots)
    own_owner = lax.dynamic_index_in_dim(owner, me, 1, keepdims=False).reshape(items)
    incoming = jnp.swapaxes(owner == me, 0, 1).reshape(nodes, items)
    outgoing = own_owner[None, :] == node_ids[:, None]
    lists = ranked(jnp.stack([outgoing, incoming]), room).reshape(2, nodes * room)
    spot = jnp.arange(nodes * room, dtype=jnp.int32)
    spot_step = nodes - 1 - ((spot // room) ^ me)
    cells = jnp.arange(items, dtype=jnp.int32)
    place = jnp.sum(
        jnp.where(lists[1][None, :] == cells[:, None], spot_step * room + spot % room, 0), axis=1
    )
    energy = 0.3 * (labels[:, 0] + 4).astype(jnp.float32) - 0.2 * labels[:, 1].astype(jnp.float32)
    smem = pl.BlockSpec(memory_space=pltpu.SMEM)
    vmem = pl.BlockSpec(memory_space=pltpu.VMEM)
    chunk = (nodes, room, levels, side, side)
    flops = 2 * 2 * count * items * levels * side**3
    residual, rayleigh = pl.pallas_call(
        functools.partial(node_kernel, (nodes, terms, shifts, slots, room, levels, side)),
        out_shape=(
            jax.ShapeDtypeStruct(vectors.shape, jnp.bfloat16),
            jax.ShapeDtypeStruct((count, side), jnp.float32),
        ),
        in_specs=[smem] * 5 + [vmem, vmem, pl.BlockSpec(memory_space=pl.ANY)],
        out_specs=(vmem, vmem),
        scratch_shapes=[
            pltpu.VMEM(left_env.shape, jnp.bfloat16),
            pltpu.VMEM((nodes,) + vectors.shape, jnp.bfloat16),
            pltpu.VMEM(chunk, jnp.bfloat16),
            pltpu.VMEM(chunk, jnp.bfloat16),
            pltpu.VMEM((nodes, room, side, count * side), jnp.float32),
            pltpu.VMEM((slots, side, count * side), jnp.float32),
            pltpu.VMEM((nodes, 8, count * side), jnp.float32),
            pltpu.SemaphoreType.DMA,
            pltpu.SemaphoreType.DMA((nodes,)),
            pltpu.SemaphoreType.DMA((2 * (nodes // 4) - 1, 4)),
            pltpu.SemaphoreType.DMA((nodes // 4,)),
            pltpu.SemaphoreType.DMA((nodes,)),
            pltpu.SemaphoreType.DMA((nodes,)),
            pltpu.SemaphoreType.DMA((nodes,)),
            pltpu.SemaphoreType.DMA((nodes,)),
        ],
        compiler_params=pltpu.CompilerParams(
            collective_id=0, has_side_effects=True, vmem_limit_bytes=VMEM_BYTES
        ),
        cost_estimate=pl.CostEstimate(
            flops=flops, bytes_accessed=2 * left_env.size * 2, transcendentals=0
        ),
    )(lists[0], lists[1], place, active.reshape(-1), energy, vectors, right_env, left_env)
    return residual, rayleigh[:, 0]


def choose(vectors, left_env, right_env, labels, partner, active):
    nodes = lax.axis_size("wf")
    items = partner.shape[0] * vectors.shape[1]
    gathered = nodes * vectors.size * 2
    even = items % nodes == 0 and nodes % 4 == 0 and nodes & (nodes - 1) == 0
    program = node_program if even and 2 * gathered < VMEM_BYTES else per_device
    return program(vectors, left_env, right_env, labels, partner, active)


def solution(mesh):
    in_specs = (
        P(None, ("grp", "wf"), None, None),
        P(None, ("grp", "wf"), None, None),
        P(None, ("grp", "wf"), None, None),
        P(("grp", "wf"), None),
        P(None, "grp"),
        P(None, ("grp", "wf")),
    )
    out_specs = (P(None, ("grp", "wf"), None, None), P("grp"))
    return jax.shard_map(
        choose, mesh=mesh, in_specs=in_specs, out_specs=out_specs, check_vma=False
    )
```

```python
import functools

import jax
import jax.numpy as jnp
from jax import lax
from jax.experimental import pallas as pl
from jax.experimental.pallas import tpu as pltpu
from jax.sharding import PartitionSpec as P

VMEM_BYTES = 56 * 2**20
STARTED = (0, 0, 3, 5, 7, 9, 11, 12, 13, 14)
WINDOW = 15


def term_parcel(flat_blocks, pack_rows, pack_keep, rows_out, per_shift):
    chosen = jnp.take(flat_blocks, pack_rows, axis=0)
    chosen = jnp.where(pack_keep[:, None, None], chosen, jnp.zeros((), chosen.dtype))
    return chosen.reshape((rows_out, per_shift) + flat_blocks.shape[1:])


def left_side(left_env, carried, vector, energy):
    summed = jnp.einsum("ksab,ksbc->sac", left_env, carried, preferred_element_type=jnp.float32)
    return summed + energy[:, None, None] * vector.astype(jnp.float32)


def per_device(vectors, left_env, right_env, labels, partner, active):
    node_count = lax.axis_size("wf")
    this_device = lax.axis_index("wf")
    vector_count = vectors.shape[0]
    slot_count = vectors.shape[1]
    block_side = vectors.shape[2]
    term_count = left_env.shape[0]
    shift_count = partner.shape[0]
    per_shift = (term_count + shift_count - 1) // shift_count
    peer_room = max(1, shift_count * slot_count // node_count)
    item_count = shift_count * slot_count
    rows_out = node_count * peer_room
    item_ids = jnp.arange(item_count, dtype=jnp.int32)
    slot_ids = jnp.arange(slot_count, dtype=jnp.int32)
    shift_ids = jnp.arange(shift_count, dtype=jnp.int32)
    own_targets = lax.dynamic_slice_in_dim(partner, this_device * slot_count, slot_count, 1)
    dest_device = (own_targets // slot_count).reshape(item_count)
    precedes = item_ids[None, :] < item_ids[:, None]
    order_rank = jnp.sum((dest_device[None, :] == dest_device[:, None]) & precedes, axis=1)
    place_device = jnp.arange(node_count, dtype=jnp.int32)[:, None, None]
    place_rank = jnp.arange(peer_room, dtype=jnp.int32)[None, :, None]
    matched = (dest_device[None, None, :] == place_device) & (
        order_rank[None, None, :] == place_rank
    )
    send_item = jnp.sum(jnp.where(matched, item_ids[None, None, :], 0), axis=2).reshape(rows_out)
    send_live = jnp.any(matched, axis=2).reshape(rows_out)
    own_blocks = this_device * slot_count + slot_ids
    block_ids = jnp.arange(partner.shape[1], dtype=jnp.int32)
    found_hits = partner[:, None, :] == own_blocks[None, :, None]
    anchor = jnp.sum(jnp.where(found_hits, block_ids[None, None, :], 0), axis=2)
    sender = anchor // slot_count
    cell_item = shift_ids[:, None] * slot_count + anchor % slot_count
    columns = sender[:, :, None] * slot_count + slot_ids[None, None, :]
    their_device = (
        jnp.take(partner, columns.reshape(-1), axis=1).reshape(
            shift_count, shift_count, slot_count, slot_count
        )
        // slot_count
    )
    their_item = shift_ids[:, None, None, None] * slot_count + slot_ids[None, None, None, :]
    before = their_item < cell_item[None, :, :, None]
    rank_cell = jnp.sum((their_device == this_device) & before, axis=(0, 3))
    recv_row = sender * peer_room + rank_cell
    term_ids = jnp.arange(term_count, dtype=jnp.int32)
    term_shift = term_ids % shift_count
    term_level = term_ids // shift_count
    level_ids = jnp.arange(per_shift, dtype=jnp.int32)
    term_grid = (send_item // slot_count)[:, None] + level_ids[None, :] * shift_count
    pack_rows = (
        jnp.minimum(term_grid, term_count - 1) * slot_count + (send_item % slot_count)[:, None]
    ).reshape(-1)
    pack_keep = (send_live[:, None] & (term_grid < term_count)).reshape(-1)
    unpack_rows = (recv_row[term_shift] * per_shift + term_level[:, None]).reshape(-1)
    energy = 0.3 * (labels[:, 0] + 4).astype(jnp.float32) - 0.2 * labels[:, 1].astype(jnp.float32)
    images = []
    keep_terms = active.astype(jnp.float32)[:, :, None, None]
    for vector_index in range(vector_count):
        product = jnp.einsum(
            "sab,ksbc->ksac", vectors[vector_index], right_env, preferred_element_type=jnp.float32
        )
        carried = (product * keep_terms).astype(jnp.bfloat16)
        parcel = term_parcel(
            carried.reshape(term_count * slot_count, block_side, block_side),
            pack_rows,
            pack_keep,
            rows_out,
            per_shift,
        )
        arrived = lax.all_to_all(parcel, "wf", split_axis=0, concat_axis=0, tiled=True)
        relocated = jnp.take(
            arrived.reshape(-1, block_side, block_side), unpack_rows, axis=0
        ).reshape(term_count, slot_count, block_side, block_side)
        images.append(left_side(left_env, relocated, vectors[vector_index], energy))
    image = jnp.stack(images)
    floats = vectors.astype(jnp.float32)
    squares = jnp.sum(floats * floats, axis=(1, 2, 3))
    correlations = jnp.sum(floats * image, axis=(1, 2, 3))
    squares_all, correlations_all = lax.psum((squares, correlations), "wf")
    rayleigh = correlations_all / (squares_all + 1e-06)
    residual = (image - rayleigh[:, None, None, None] * floats).astype(jnp.bfloat16)
    return (residual, rayleigh)


def ranked(hits, room):
    rank = jnp.cumsum(hits.astype(jnp.int32), axis=-1) - 1
    item_ids = jnp.arange(hits.shape[-1], dtype=jnp.int32)
    level = jnp.arange(room, dtype=jnp.int32)[:, None]
    matched = hits[..., None, :] & (rank[..., None, :] == level)
    return jnp.sum(jnp.where(matched, item_ids, 0), axis=-1)


def peer_of(me, step, nodes):
    difference = nodes - 1 - step
    peer, bit = 0, 1
    while bit < nodes:
        peer += ((me // bit + difference // bit) % 2) * bit
        bit *= 2
    return peer


def node_kernel(
    sizes,
    send_item,
    recv_cell,
    place,
    active,
    energy,
    v_ref,
    r_ref,
    l_hbm,
    out_ref,
    ray_ref,
    l_ref,
    vall,
    parcel,
    arrived,
    partial,
    images,
    stats,
    l_sem,
    v_recv,
    v_send,
    y_send,
    r_recv,
    r_send,
    s_recv,
    s_send,
):
    nodes, terms, shifts, slots, room, levels, side = sizes
    z_count = nodes // 4
    steps = nodes - 1
    me = lax.axis_index("wf")
    z, y, core = me // 4, (me // 2) % 2, me % 2
    l_copy = pltpu.make_async_copy(l_hbm, l_ref, l_sem)
    l_copy.start()

    barrier = pltpu.get_barrier_semaphore()

    def greet(step, carry):
        pl.semaphore_signal(barrier, inc=1, device_id={"wf": peer_of(me, step, nodes)})
        return carry

    lax.fori_loop(0, steps, greet, 0)
    pl.semaphore_wait(barrier, steps)

    def v_copy(chunk, target, send_sem, half):
        return pltpu.make_async_remote_copy(
            src_ref=vall.at[chunk, half],
            dst_ref=vall.at[chunk, half],
            send_sem=send_sem.at[half],
            recv_sem=v_recv.at[chunk, half],
            device_id={"wf": target},
        )

    y_peer = z * 4 + (1 - y) * 2 + core
    core_peer = z * 4 + y * 2 + (1 - core)
    up, down = (me + 4) % nodes, (me + nodes - 4) % nodes

    def wait_chunk(chunk, half):
        v_copy(chunk, core_peer, y_send.at[0], half).wait_recv()

    def each_way(dz, half, action):
        index = dz + z_count - 1
        chunk = me + 4 * dz
        if dz <= 0:

            @pl.when(z < z_count - 1)
            def _():
                action(v_copy(chunk, up, v_send.at[index, 0], half))

        if dz >= 0:

            @pl.when(z > 0)
            def _():
                action(v_copy(chunk, down, v_send.at[index, 1], half))

        action(v_copy(chunk, y_peer, v_send.at[index, 2], half))
        action(v_copy(chunk, core_peer, v_send.at[index, 3], half))

    def y_chunk(z_step):
        return ((z + z_step) % z_count) * 4 + (1 - y) * 2 + core

    def r_copy(step):
        return pltpu.make_async_remote_copy(
            src_ref=parcel.at[step],
            dst_ref=arrived.at[step],
            send_sem=r_send.at[step],
            recv_sem=r_recv.at[step],
            device_id={"wf": peer_of(me, step, nodes)},
        )

    def pack(step, buffer):
        peer = peer_of(me, step, nodes)
        for index in range(room):
            item = send_item[peer * room + index]
            shift, slot = item // slots, item % slots
            for level in range(levels):
                term = shift + level * shifts
                live = (term < terms).astype(jnp.int32)
                term = jnp.minimum(term, terms - 1)
                keep = (active[term * slots + slot] * live).astype(jnp.float32)
                block = r_ref[term, slot].astype(jnp.float32) * keep
                buffer[step, index, level] = block.astype(jnp.bfloat16)

    def pack_and_send(step, carry):
        pack(step, parcel)
        r_copy(step).start()
        return carry

    def send(turn, carry):
        step = steps - 1 - turn

        @pl.when(turn >= WINDOW)
        def _():
            r_copy(step + WINDOW).wait_send()

        pack(step, parcel)
        r_copy(step).start()
        return carry

    def inside(dz):
        return (z + dz >= 0) & (z + dz < z_count)

    def relay(far, half):
        for dz in (-far, far):

            @pl.when(inside(dz))
            def _(dz=dz):
                wait_chunk(me + 4 * dz, half)
                each_way(dz, half, lambda copy: copy.start())

    def pass_on(z_step):
        chunk = y_chunk(z_step)
        for half in range(2):
            wait_chunk(chunk, half)
            v_copy(chunk, core_peer, y_send.at[z_step], half).start()

    others = [sign * far for far in range(1, z_count) for sign in (-1, 1)]
    events = [functools.partial(relay, far, half) for far in range(1, z_count) for half in range(2)]
    events += [functools.partial(pass_on, z_step) for z_step in range(z_count)]
    vall[me] = v_ref[...]
    for half in range(2):
        each_way(0, half, lambda copy: copy.start())
    begun = 0
    for number, event in enumerate(events):
        goal = min(steps, STARTED[number]) if number < len(STARTED) else steps
        lax.fori_loop(begun, goal, send, 0)
        begun = goal
        event()
    lax.fori_loop(begun, steps, send, 0)
    pack(steps, arrived)

    def last_chunks(z_step, carry):
        z_from = (z + z_step) % z_count
        for half in range(2):
            wait_chunk(z_from * 4 + y * 2 + (1 - core), half)
            wait_chunk(z_from * 4 + (1 - y) * 2 + (1 - core), half)
        return carry

    lax.fori_loop(0, z_count, last_chunks, 0)
    l_copy.wait()

    def multiply(step):
        peer = peer_of(me, step, nodes)

        def one(index, carry):
            cell = recv_cell[peer * room + index]
            shift, slot = cell // slots, cell % slots
            pair = jnp.concatenate([vall[peer, 0, slot], vall[peer, 1, slot]], axis=0)
            total = jnp.zeros((side, 2 * side), jnp.float32)
            for level in range(levels):
                term = jnp.minimum(shift + level * shifts, terms - 1)
                carried = jnp.dot(
                    pair, arrived[step, index, level], preferred_element_type=jnp.float32
                ).astype(jnp.bfloat16)
                both = jnp.concatenate([carried[:side], carried[side:]], axis=1)
                total += jnp.dot(l_ref[term, slot], both, preferred_element_type=jnp.float32)
            partial[step, index] = total
            return carry

        lax.fori_loop(0, room, one, 0)

    multiply(steps)

    def take(back, carry):
        step = steps - 1 - back
        r_copy(step).wait_recv()
        multiply(step)
        return carry

    lax.fori_loop(0, steps, take, 0)

    def total_slot(slot, carry):
        image = jnp.zeros((side, 2 * side), jnp.float32)
        for shift in range(shifts):
            spot = place[shift * slots + slot]
            image += partial[spot // room, spot % room]
        own = jnp.concatenate([v_ref[0, slot], v_ref[1, slot]], axis=1).astype(jnp.float32)
        image += energy[slot] * own
        images[slot] = image
        squares = jnp.sum(own * own, axis=0, keepdims=True)
        correlations = jnp.sum(own * image, axis=0, keepdims=True)
        return (carry[0] + squares, carry[1] + correlations)

    blank = jnp.zeros((1, 2 * side), jnp.float32)
    squares, correlations = lax.fori_loop(0, slots, total_slot, (blank, blank))
    row = lax.broadcasted_iota(jnp.int32, (8, 2 * side), 0)
    stats[me] = jnp.where(row == 0, squares, jnp.where(row == 1, correlations, 0.0))

    def s_copy(chunk, step):
        return pltpu.make_async_remote_copy(
            src_ref=stats.at[chunk],
            dst_ref=stats.at[chunk],
            send_sem=s_send.at[step],
            recv_sem=s_recv.at[chunk],
            device_id={"wf": peer_of(me, step, nodes)},
        )

    def share(step, carry):
        s_copy(me, step).start()
        return carry

    lax.fori_loop(0, steps, share, 0)

    def hear(step, carry):
        s_copy(peer_of(me, step, nodes), step).wait_recv()
        return carry

    lax.fori_loop(0, steps, hear, 0)
    sums = stats[0]
    for node in range(1, nodes):
        sums += stats[node]
    quotients = []
    for vector in range(2):
        lanes = slice(vector * side, (vector + 1) * side)
        square = jnp.sum(sums[0:1, lanes], axis=1, keepdims=True)
        correlation = jnp.sum(sums[1:2, lanes], axis=1, keepdims=True)
        quotient = correlation / (square + 1e-06)
        quotients.append(jnp.broadcast_to(quotient, (1, side)))
    ray_ref[...] = jnp.concatenate(quotients, axis=0)
    factor = jnp.concatenate(quotients, axis=1)

    def finish(slot, carry):
        own = jnp.concatenate([v_ref[0, slot], v_ref[1, slot]], axis=1).astype(jnp.float32)
        result = (images[slot] - factor * own).astype(jnp.bfloat16)
        out_ref[0, slot] = result[:, :side]
        out_ref[1, slot] = result[:, side:]
        return carry

    lax.fori_loop(0, slots, finish, 0)

    for half in range(2):
        each_way(0, half, lambda copy: copy.wait_send())
    for dz in others:

        @pl.when(inside(dz))
        def _(dz=dz):
            for half in range(2):
                each_way(dz, half, lambda copy: copy.wait_send())

    def sent_y(z_step, carry):
        for half in range(2):
            v_copy(y_chunk(z_step), core_peer, y_send.at[z_step], half).wait_send()
        return carry

    lax.fori_loop(0, z_count, sent_y, 0)

    def sent(step, carry):
        s_copy(me, step).wait_send()

        @pl.when(step < min(WINDOW, steps))
        def _():
            r_copy(step).wait_send()

        return carry

    lax.fori_loop(0, steps, sent, 0)


def node_program(vectors, left_env, right_env, labels, partner, active):
    nodes = lax.axis_size("wf")
    me = lax.axis_index("wf")
    count, slots, side = vectors.shape[:3]
    terms, shifts = left_env.shape[0], partner.shape[0]
    levels = (terms + shifts - 1) // shifts
    items = shifts * slots
    room = items // nodes
    node_ids = jnp.arange(nodes, dtype=jnp.int32)
    owner = (partner // slots).reshape(shifts, nodes, slots)
    own_owner = lax.dynamic_index_in_dim(owner, me, 1, keepdims=False).reshape(items)
    incoming = jnp.swapaxes(owner == me, 0, 1).reshape(nodes, items)
    outgoing = own_owner[None, :] == node_ids[:, None]
    lists = ranked(jnp.stack([outgoing, incoming]), room).reshape(2, nodes * room)
    spot = jnp.arange(nodes * room, dtype=jnp.int32)
    spot_step = nodes - 1 - ((spot // room) ^ me)
    cells = jnp.arange(items, dtype=jnp.int32)
    place = jnp.sum(
        jnp.where(lists[1][None, :] == cells[:, None], spot_step * room + spot % room, 0), axis=1
    )
    energy = 0.3 * (labels[:, 0] + 4).astype(jnp.float32) - 0.2 * labels[:, 1].astype(jnp.float32)
    smem = pl.BlockSpec(memory_space=pltpu.SMEM)
    vmem = pl.BlockSpec(memory_space=pltpu.VMEM)
    chunk = (nodes, room, levels, side, side)
    flops = 2 * 2 * count * items * levels * side**3
    residual, rayleigh = pl.pallas_call(
        functools.partial(node_kernel, (nodes, terms, shifts, slots, room, levels, side)),
        out_shape=(
            jax.ShapeDtypeStruct(vectors.shape, jnp.bfloat16),
            jax.ShapeDtypeStruct((count, side), jnp.float32),
        ),
        in_specs=[smem] * 5 + [vmem, vmem, pl.BlockSpec(memory_space=pl.ANY)],
        out_specs=(vmem, vmem),
        scratch_shapes=[
            pltpu.VMEM(left_env.shape, jnp.bfloat16),
            pltpu.VMEM((nodes,) + vectors.shape, jnp.bfloat16),
            pltpu.VMEM(chunk, jnp.bfloat16),
            pltpu.VMEM(chunk, jnp.bfloat16),
            pltpu.VMEM((nodes, room, side, count * side), jnp.float32),
            pltpu.VMEM((slots, side, count * side), jnp.float32),
            pltpu.VMEM((nodes, 8, count * side), jnp.float32),
            pltpu.SemaphoreType.DMA,
            pltpu.SemaphoreType.DMA((nodes, 2)),
            pltpu.SemaphoreType.DMA((2 * (nodes // 4) - 1, 4, 2)),
            pltpu.SemaphoreType.DMA((nodes // 4, 2)),
            pltpu.SemaphoreType.DMA((nodes,)),
            pltpu.SemaphoreType.DMA((nodes,)),
            pltpu.SemaphoreType.DMA((nodes,)),
            pltpu.SemaphoreType.DMA((nodes,)),
        ],
        compiler_params=pltpu.CompilerParams(
            collective_id=0, has_side_effects=True, vmem_limit_bytes=VMEM_BYTES
        ),
        cost_estimate=pl.CostEstimate(
            flops=flops, bytes_accessed=2 * left_env.size * 2, transcendentals=0
        ),
    )(lists[0], lists[1], place, active.reshape(-1), energy, vectors, right_env, left_env)
    return residual, rayleigh[:, 0]


def choose(vectors, left_env, right_env, labels, partner, active):
    nodes = lax.axis_size("wf")
    items = partner.shape[0] * vectors.shape[1]
    gathered = nodes * vectors.size * 2
    even = items % nodes == 0 and nodes % 4 == 0 and nodes & (nodes - 1) == 0
    program = node_program if even and 2 * gathered < VMEM_BYTES else per_device
    return program(vectors, left_env, right_env, labels, partner, active)


def solution(mesh):
    in_specs = (
        P(None, ("grp", "wf"), None, None),
        P(None, ("grp", "wf"), None, None),
        P(None, ("grp", "wf"), None, None),
        P(("grp", "wf"), None),
        P(None, "grp"),
        P(None, ("grp", "wf")),
    )
    out_specs = (P(None, ("grp", "wf"), None, None), P("grp"))
    return jax.shard_map(
        choose, mesh=mesh, in_specs=in_specs, out_specs=out_specs, check_vma=False
    )
```
